32 devices in a mesh: patch: 2 (over y), space: 4 (over z), tm: 2 (over x), row: 2 (over core).
Axes of the slice: x: 2, y: 2, z: 4, core: 2. Of those that a mesh axis runs over, the one named last changes fastest.
Arguments:
- doppler: float32 [32, 192, 256], P('tm', ('patch', 'space'), 'row'), parts along dimension 1, may hold values from -24 to 24
- cycle_masks: int32 [8, 33, 33], replicated, may hold values from 0 to 1, as said below
- lag_list: int32 [4], replicated, may hold values from 1 to 16, as said below
Outputs:
- correlations: float32 [2, 8, 4, 192, 256], P('tm', None, None, ('patch', 'space'), 'row'), parts along dimension 3
The draws below stay inside these ranges and needn't reach their ends.
There are 2 independent parts, one for each index of `patch`. The reference program is written for one: setup_inputs(seed, part) draws one part's arguments, and reference() takes and returns one part's arrays. A program takes and returns all parts, laid end to end along the dimension named above; an argument that names none is the same for every part. Nothing has to cross between parts.
Inputs may be any that keep to these rules, and one draw needn't show every extreme that they name: Each cycle_masks[r] is 1 only at offsets whose distance from the centre lies within half a pixel of one radius of 1 to 16, distinct radii over r, and is 1 at the offsets of that radius along both pixel directions; one annulus has radius 16. `lag_list`: the lags are distinct and one of them is 16.
All inputs are finite; a program needn't handle non-finite values.
Results may differ from the reference program's by a relative error of at most 0.0033.
Values may be sent and summed in bfloat16 or wider, within the bound.
A program may use at most 64 MiB of HBM per device.

```python
import jax
import jax.numpy as jnp
from jax import lax

F_DEV = 16
RADII = 8
RMAX = 16
LAGS = 4
MAXLAG = 16
FRAMES = 32
COLS = 96
ROWS = 256
WINDOWS = 2


def cycle_radii(key):
    others = jax.random.permutation(jax.random.fold_in(key, 11), RMAX - 1)[:RADII - 1] + 1
    listed = jnp.concatenate([jnp.full((1,), RMAX, jnp.int32), others.astype(jnp.int32)])
    return listed[jax.random.permutation(jax.random.fold_in(key, 12), RADII)]


def draw_cycle_masks(key, part):
    radii = cycle_radii(key)
    width = 2 * RMAX + 1
    offset = jnp.arange(width, dtype=jnp.int32) - RMAX
    distance = 4 * (offset[:, None] * offset[:, None] + offset[None, :] * offset[None, :])
    lower = (2 * radii - 1) * (2 * radii - 1)
    upper = (2 * radii + 1) * (2 * radii + 1)
    inside = (distance[None] >= lower[:, None, None]) & (distance[None] < upper[:, None, None])
    keeping = jax.random.randint(jax.random.fold_in(key, 13), (RADII, width, width), 0, 4) > 0
    along_first = (offset[None, :, None] == radii[:, None, None]) & (offset[None, None, :] == 0)
    along_second = (offset[None, :, None] == 0) & (offset[None, None, :] == radii[:, None, None])
    return (inside & keeping | along_first | along_second).astype(jnp.int32)


def draw_lag_list(key, part):
    others = jax.random.permutation(jax.random.fold_in(key, 21), MAXLAG - 1)[:LAGS - 1] + 1
    listed = jnp.concatenate([jnp.full((1,), MAXLAG, jnp.int32), others.astype(jnp.int32)])
    return listed[jax.random.permutation(jax.random.fold_in(key, 22), LAGS)]


def block_scale(key, extent, cuts, smallest, top_value):
    def one(dim, shards_of):
        heights = jax.random.uniform(jax.random.fold_in(jax.random.fold_in(key, 6), dim), (shards_of,), jnp.float32, smallest / len(cuts), top_value / len(cuts))
        return jnp.repeat(jnp.exp(heights), extent[dim] // shards_of).reshape((-1,) + (1,) * (len(extent) - dim - 1))

    factor_of = one(*cuts[0])
    for cut in cuts[1:]:
        factor_of = factor_of * one(*cut)
    return factor_of


def scatter_about(own_key, dims, scale, bound, cuts=(), held_as=jnp.bfloat16):
    gain = block_scale(own_key, dims, cuts, -0.22, 0.18) if cuts else 1.0
    array = jax.random.normal(own_key, dims, jnp.float32) * scale * gain
    return jnp.minimum(jnp.maximum(array, -bound), bound).astype(held_as)


def setup_inputs(seed: int = 0, part: int = 0) -> dict:
    streams_of = jax.random.split(jax.random.key(seed), 4)
    part_keys = jax.random.split(jax.random.fold_in(streams_of[3], part), 4)
    doppler = scatter_about(part_keys[0], (FRAMES, COLS, ROWS), 4.0, 24.0, ((0, 2), (1, 4), (2, 2)), jnp.float32)
    cycle_masks = draw_cycle_masks(jax.random.fold_in(streams_of[3], 71), part)
    lag_list = draw_lag_list(jax.random.fold_in(streams_of[3], 71), part)
    return {"doppler": doppler, "cycle_masks": cycle_masks, "lag_list": lag_list}


gaussian_taps = (0.05448868, 0.24420134, 0.40261995, 0.24420134, 0.05448868)


def gaussian_blur(field, axis_dim, cell_count):
    summed = gaussian_taps[0] * lax.slice_in_dim(field, 0, cell_count, axis=axis_dim)
    for shift_index in range(1, len(gaussian_taps)):
        summed = summed + gaussian_taps[shift_index] * lax.slice_in_dim(field, shift_index, shift_index + cell_count, axis=axis_dim)
    return summed


def reference(doppler, cycle_masks, lag_list):
    blur_reach = len(gaussian_taps) // 2
    padded = jnp.pad(doppler, ((0, 0), (blur_reach, blur_reach), (blur_reach, blur_reach)))
    smooth = gaussian_blur(gaussian_blur(padded, 1, COLS), 2, ROWS).astype(jnp.bfloat16)
    kernel = cycle_masks.astype(jnp.float32)[:, None, :, :]
    counts = jnp.sum(cycle_masks, axis=(1, 2)).astype(jnp.float32)
    history = jnp.concatenate([jnp.zeros((MAXLAG, COLS, ROWS), smooth.dtype), smooth], 0)

    def window_corr(window_index):
        frame_start = (window_index * F_DEV).astype(jnp.int32)
        own_frames = lax.dynamic_slice_in_dim(smooth, frame_start, F_DEV, 0).astype(jnp.float32)
        cycle_sums = lax.conv_general_dilated(own_frames[:, None], kernel, (1, 1), ((RMAX, RMAX), (RMAX, RMAX)), dimension_numbers=("NCHW", "OIHW", "NCHW"), precision=lax.Precision.HIGHEST)
        annulus = cycle_sums / counts[None, :, None, None]
        earlier = jax.vmap(lambda lag_value: lax.dynamic_slice_in_dim(history, (MAXLAG + frame_start - lag_value).astype(jnp.int32), F_DEV, 0))(lag_list).astype(jnp.float32)
        return jnp.einsum("ltcx,trcx->rlcx", earlier, annulus, precision=lax.Precision.HIGHEST)

    return lax.map(window_corr, jnp.arange(WINDOWS, dtype=jnp.int32))
```

```python
import functools

import jax
import jax.numpy as jnp
from jax import lax
from jax.experimental import pallas as pl
from jax.experimental.pallas import tpu as pltpu
from jax.sharding import PartitionSpec as P

MESH = pl.DeviceIdType.MESH
RMAX = 16
LANES = 128
TILE = 32
SPAN = 2 * TILE
PACK = LANES // TILE
gaussian_taps = (0.05448868, 0.24420134, 0.40261995, 0.24420134, 0.05448868)
REACH = len(gaussian_taps) // 2


def lane_iota(shape):
    return lax.broadcasted_iota(jnp.int32, shape, len(shape) - 1)


def pack_borders(blocks, side):
    group = lane_iota(blocks[0].shape) // TILE
    base = (1 - side) * TILE
    packed = None
    for k, block in enumerate(blocks):
        turned = pltpu.roll(block, lax.rem(k * TILE + base, LANES), 1)
        packed = turned if packed is None else jnp.where(group == k, turned, packed)
    return packed


def unpack_border(packed, k, side):
    base = side * (LANES - TILE)
    turned = pltpu.roll(packed, lax.rem(LANES - k * TILE + base, LANES), 1)
    lane = lane_iota(packed.shape)
    return jnp.where((lane >= base) & (lane < base + TILE), turned, jnp.zeros_like(turned))


def exchange_body(frames, cols, dop, field, halo, series, wide, packs, packed16, halo_in, unpacked,
                  natural, send, recv):
    count_s, count_t = lax.axis_size("space"), lax.axis_size("tm")
    s, t, side = lax.axis_index("space"), lax.axis_index("tm"), lax.axis_index("row")
    has_lo, has_hi = s > 0, s < count_s - 1
    has_pr, has_nx = t > 0, t < count_t - 1
    lo, hi = {"space": s - 1}, {"space": s + 1}
    lo_x, hi_x = {"space": s - 1, "row": 1 - side}, {"space": s + 1, "row": 1 - side}
    partner = {"row": 1 - side}
    prev, nxt = {"tm": t - 1}, {"tm": t + 1}
    groups = cols // PACK
    reach_groups = RMAX // PACK
    top = RMAX + cols
    sent = frames * cols
    always = None

    def when(cond, act):
        if cond is None:
            act()
        else:
            pl.when(cond)(act)

    barrier = pltpu.get_barrier_semaphore()

    def greet(*devices):
        def act():
            for device in devices:
                pl.semaphore_signal(barrier, inc=1, device_id=device, device_id_type=MESH)
        return act

    greet(partner)()
    pl.when(has_lo)(greet(lo, lo_x))
    pl.when(has_hi)(greet(hi, hi_x))
    pl.when(has_pr)(greet(prev))
    pl.when(has_nx)(greet(nxt))

    for c in range(cols):
        wide[REACH + c] = dop[pl.ds(c, frames, stride=cols), :]
    for g in range(groups):
        packs[g] = pack_borders([wide[REACH + g * PACK + k] for k in range(PACK)], side)

    def zero(ref, start, size):
        def act():
            ref[pl.ds(start, size)] = jnp.zeros((size,) + ref.shape[1:], ref.dtype)
        return act

    no_lo, no_hi, no_pr = s == 0, s == count_s - 1, t == 0
    field[pl.ds(top + RMAX, 1)] = jnp.zeros((1, frames, LANES), field.dtype)
    for cond, low in ((no_lo, True), (no_hi, False)):
        pl.when(cond)(zero(wide, 0 if low else REACH + cols, REACH))
        pl.when(cond)(zero(halo_in, 0 if low else groups + 1, 1))
        pl.when(cond)(zero(field, 0 if low else top, RMAX))
        pl.when(cond)(zero(halo, 0 if low else reach_groups + groups, reach_groups))
    pl.when(no_pr)(zero(series, 0, sent))

    def copy(index, source, target, device):
        return pltpu.make_async_remote_copy(
            src_ref=source, dst_ref=target, send_sem=send.at[index], recv_sem=recv.at[index],
            device_id=device, device_id_type=MESH,
        )

    first = [
        (copy(0, wide.at[pl.ds(REACH, REACH)], wide.at[pl.ds(REACH + cols, REACH)], lo), has_lo, has_hi),
        (copy(1, wide.at[pl.ds(cols, REACH)], wide.at[pl.ds(0, REACH)], hi), has_hi, has_lo),
        (copy(2, packs, halo_in.at[pl.ds(1, groups)], partner), always, always),
        (copy(3, packs.at[pl.ds(0, 1)], halo_in.at[pl.ds(groups + 1, 1)], lo_x), has_lo, has_hi),
        (copy(4, packs.at[pl.ds(groups - 1, 1)], halo_in.at[pl.ds(0, 1)], hi_x), has_hi, has_lo),
    ]
    second = [
        (copy(5, field.at[pl.ds(RMAX, RMAX)], field.at[pl.ds(top, RMAX)], lo), has_lo, has_hi),
        (copy(6, field.at[pl.ds(cols, RMAX)], field.at[pl.ds(0, RMAX)], hi), has_hi, has_lo),
        (copy(7, packed16, halo.at[pl.ds(reach_groups, groups)], partner), always, always),
        (copy(8, packed16.at[pl.ds(0, reach_groups)],
              halo.at[pl.ds(reach_groups + groups, reach_groups)], lo_x), has_lo, has_hi),
        (copy(9, packed16.at[pl.ds(groups - reach_groups, reach_groups)],
              halo.at[pl.ds(0, reach_groups)], hi_x), has_hi, has_lo),
        (copy(10, series.at[pl.ds(sent, sent)], series.at[pl.ds(0, sent)], nxt), has_nx, has_pr),
    ]

    met = lambda flag: jnp.where(flag, 1, 0).astype(jnp.int32)
    pl.semaphore_wait(barrier, 1 + 2 * met(has_lo) + 2 * met(has_hi) + met(has_pr) + met(has_nx))
    for moved, sends, _ in first:
        when(sends, moved.start)
    for moved, _, receives in first:
        when(receives, moved.wait_recv)

    for i in range(cols + 2 * REACH):
        place = i + PACK - REACH
        unpacked[i] = unpack_border(halo_in[place // PACK], place % PACK, side)
    lane = lane_iota((frames, LANES))
    for g in range(groups):
        smoothed = []
        for k in range(PACK):
            c = g * PACK + k
            own, other = [
                functools.reduce(lambda a, b: a + b, [gaussian_taps[i] * ref[c + i] for i in range(len(gaussian_taps))])
                for ref in (wide, unpacked)
            ]
            total = None
            for i, tap in enumerate(gaussian_taps):
                shift = i - REACH
                if shift > 0:
                    moved = pltpu.roll(jnp.where(lane < shift, other, own), LANES - shift, 1)
                elif shift < 0:
                    moved = pltpu.roll(jnp.where(lane >= LANES + shift, other, own), -shift, 1)
                else:
                    moved = own
                total = tap * moved if total is None else total + tap * moved
            smoothed.append(total)
            field[RMAX + c] = total.astype(field.dtype)
            natural[pl.ds(c, frames, stride=cols), :] = total
        packed16[g] = pack_borders(smoothed, side).astype(packed16.dtype)
    series[pl.ds(sent, sent)] = natural[...].astype(series.dtype)

    for moved, sends, _ in second:
        when(sends, moved.start)
    for moved, sends, _ in first:
        when(sends, moved.wait_send)
    for moved, _, receives in second:
        when(receives, moved.wait_recv)
    for moved, sends, _ in second:
        when(sends, moved.wait_send)


def build_bands(radii, width, mask, bands):
    for q in range(TILE):
        for block in range(width // LANES):
            piece = mask[:, pl.ds(block * LANES, LANES)]
            bands[block, pl.ds(q, radii, stride=TILE), :] = piece if q == 0 else pltpu.roll(piece, q, 1)


def correlate_body(frames, cols, radii, lags, lag_list, mask, field, halo, series, out, bands, windows,
                   sums, spread, parts):
    side = lax.axis_index("row")
    tiles = LANES // TILE
    width = mask.shape[1]
    pairs = width // LANES
    build_bands(radii, width, mask, bands)

    lane = lane_iota((frames, LANES))
    previous = [None] * tiles
    f32 = jnp.float32
    total_cols = cols + 2 * RMAX
    for i in range(total_cols + 1):
        own = field[i].astype(f32)
        if i < total_cols:
            other = unpack_border(halo[i // PACK].astype(f32), i % PACK, side)
        else:
            other = jnp.zeros_like(own)
        for j in range(tiles):
            source = own
            if j == 0:
                source = jnp.where(lane >= LANES - RMAX, other, own)
            if j == tiles - 1:
                source = jnp.where(lane < RMAX, other, source)
            shift = (RMAX - TILE * j) % LANES
            odd = pltpu.roll(source, (shift + SPAN) % LANES, 1)
            if i > 0:
                windows[j, i - 1] = jnp.where(lane < SPAN, previous[j], odd).astype(jnp.bfloat16)
            if i < total_cols:
                previous[j] = pltpu.roll(source, shift, 1)

    rows = lax.broadcasted_iota(jnp.int32, (LANES, tiles * LANES), 0)
    places = lax.broadcasted_iota(jnp.int32, (LANES, tiles * LANES), 1)
    pick = jnp.where(rows == (places // LANES) * TILE + places % TILE, 1.0, 0.0).astype(jnp.bfloat16)
    spread[...] = jnp.dot(series[...], pick, preferred_element_type=f32)

    weights = jnp.concatenate([bands[g].astype(jnp.bfloat16) for g in range(pairs)], axis=1)
    halves = radii * TILE // LANES
    for j in range(tiles):
        left = jnp.concatenate(
            [windows[j, pl.ds(2 * g, cols)].reshape(cols * frames, LANES) for g in range(pairs)], axis=1
        )
        total = lax.dot_general(left, weights, (((1,), (1,)), ((), ())), preferred_element_type=f32)
        for h in range(halves):
            sums[j, h] = total[:, h * LANES : (h + 1) * LANES]

    starts = [frames - lag_list[l] for l in range(lags)]
    for j in range(tiles):
        totals = [[None] * halves for _ in range(lags)]
        for t in range(frames):
            annulus = [sums[j, h, pl.ds(t, cols, stride=frames), :] for h in range(halves)]
            for l in range(lags):
                begin = pl.multiple_of((starts[l] + t) * cols, 8)
                earlier = spread[pl.ds(begin, cols), pl.ds(j * LANES, LANES)]
                for h in range(halves):
                    term = earlier * annulus[h]
                    totals[l][h] = term if t == 0 else totals[l][h] + term
        for l in range(lags):
            for h in range(halves):
                parts[j, l, h] = totals[l][h]

    counts = jnp.sum(mask[...], axis=1, keepdims=True)
    group = lane_iota((cols, LANES)) // TILE
    for r in range(radii):
        h, rr = r // PACK, r % PACK
        count = counts[r : r + 1, 0:1]
        for l in range(lags):
            whole = None
            for j in range(tiles):
                shift = (TILE * (j - rr)) % LANES
                piece = parts[j, l, h]
                piece = pltpu.roll(piece, shift, 1) if shift else piece
                whole = piece if whole is None else jnp.where(group == j, piece, whole)
            out[r, l] = whole / count


def local(doppler, cycle_masks, lag_list):
    frames, cols, rows = doppler.shape
    radii, side = cycle_masks.shape[:2]
    lags = lag_list.shape[0]
    assert rows == LANES and frames == RMAX and side == 2 * RMAX + 1 and cols % 8 == 0 and cols >= RMAX
    assert lax.axis_size("row") == 2 and radii * TILE % LANES == 0
    mask = jnp.pad(cycle_masks.astype(jnp.float32), ((0, 0), (0, side % 2), (0, SPAN - side)))
    mask = mask.reshape(radii, -1)
    groups = cols // PACK
    ext = cols + 2 * RMAX
    f32, bf16 = jnp.float32, jnp.bfloat16
    vmem = pl.BlockSpec(memory_space=pltpu.VMEM)
    field, halo, series = pl.pallas_call(
        functools.partial(exchange_body, frames, cols),
        out_shape=(
            jax.ShapeDtypeStruct((ext + 1, frames, LANES), bf16),
            jax.ShapeDtypeStruct((ext // PACK, frames, LANES), bf16),
            jax.ShapeDtypeStruct((2 * frames * cols, LANES), bf16),
        ),
        in_specs=[vmem],
        out_specs=(vmem, vmem, vmem),
        scratch_shapes=[
            pltpu.VMEM((cols + 2 * REACH, frames, LANES), f32),
            pltpu.VMEM((groups, frames, LANES), f32),
            pltpu.VMEM((groups, frames, LANES), bf16),
            pltpu.VMEM((groups + 2, frames, LANES), f32),
            pltpu.VMEM((cols + 2 * REACH, frames, LANES), f32),
            pltpu.VMEM((frames * cols, LANES), f32),
            pltpu.SemaphoreType.DMA((11,)),
            pltpu.SemaphoreType.DMA((11,)),
        ],
        compiler_params=pltpu.CompilerParams(
            collective_id=0, has_side_effects=True, vmem_limit_bytes=32 * 2**20
        ),
    )(doppler.reshape(frames * cols, LANES))
    tiles = LANES // TILE
    out = pl.pallas_call(
        functools.partial(correlate_body, frames, cols, radii, lags),
        out_shape=jax.ShapeDtypeStruct((radii, lags, cols, LANES), f32),
        in_specs=[pl.BlockSpec(memory_space=pltpu.SMEM), vmem, vmem, vmem, vmem],
        out_specs=vmem,
        scratch_shapes=[
            pltpu.VMEM((mask.shape[1] // LANES, radii * TILE, LANES), f32),
            pltpu.VMEM((tiles, ext, frames, LANES), bf16),
            pltpu.VMEM((tiles, radii * TILE // LANES, cols * frames, LANES), f32),
            pltpu.VMEM((2 * frames * cols, tiles * LANES), f32),
            pltpu.VMEM((tiles, lags, radii * TILE // LANES, cols, LANES), f32),
        ],
        compiler_params=pltpu.CompilerParams(vmem_limit_bytes=48 * 2**20),
    )(lag_list, mask, field, halo, series)
    return out[None]


def solution(mesh):
    return jax.shard_map(
        local,
        mesh=mesh,
        in_specs=(P("tm", ("patch", "space"), "row"), P(), P()),
        out_specs=P("tm", None, None, ("patch", "space"), "row"),
        check_vma=False,
    )
```

```python
import functools

import jax
import jax.numpy as jnp
from jax import lax
from jax.experimental import pallas as pl
from jax.experimental.pallas import tpu as pltpu
from jax.sharding import PartitionSpec as P

MESH = pl.DeviceIdType.MESH
RMAX = 16
LANES = 128
TILE = 32
SPAN = 2 * TILE
PACK = LANES // TILE
gaussian_taps = (0.05448868, 0.24420134, 0.40261995, 0.24420134, 0.05448868)
REACH = len(gaussian_taps) // 2
VMEM_SHARE = 24 * 2**20


def lane_iota(shape):
    return lax.broadcasted_iota(jnp.int32, shape, len(shape) - 1)


def pack_borders(blocks, side):
    group = lane_iota(blocks[0].shape) // TILE
    base = (1 - side) * TILE
    packed = None
    for k, block in enumerate(blocks):
        turned = pltpu.roll(block, lax.rem(k * TILE + base, LANES), 1)
        packed = turned if packed is None else jnp.where(group == k, turned, packed)
    return packed


def unpack_border(packed, k, side):
    base = side * (LANES - TILE)
    turned = pltpu.roll(packed, lax.rem(LANES - k * TILE + base, LANES), 1)
    lane = lane_iota(packed.shape)
    return jnp.where((lane >= base) & (lane < base + TILE), turned, jnp.zeros_like(turned))


def build_weights(radii, mask_in, bands, weights, counts):
    side = mask_in.shape[0]
    pairs = weights.shape[0] // LANES
    bits = mask_in[...].astype(jnp.float32).reshape(side * radii, side).astype(jnp.bfloat16)
    rows = lax.broadcasted_iota(jnp.int32, (side, LANES), 0)
    lane = lane_iota((side, LANES))
    put = [jnp.where(lane == rows + k * SPAN, 1.0, 0.0).astype(jnp.bfloat16) for k in range(2)]
    even, odd = [jnp.dot(bits, p, preferred_element_type=jnp.float32) for p in put]
    total = None
    for g in range(pairs):
        a = 2 * g
        piece = even[a * radii : (a + 1) * radii]
        if a + 1 < side:
            piece = piece + odd[(a + 1) * radii : (a + 2) * radii]
        total = piece if total is None else total + piece
        for q in range(TILE):
            bands[g, pl.ds(q, radii, stride=TILE), :] = pltpu.roll(piece, q, 1) if q else piece
        weights[pl.ds(g * LANES, LANES), :] = bands[g].T.astype(weights.dtype)
    counts[...] = jnp.broadcast_to(jnp.sum(total, axis=1, keepdims=True), counts.shape)


def build_windows(places, frames, total_cols, side, field, halo, windows):
    lane = lane_iota((frames, LANES))
    tiles = windows.shape[0]
    sources = {}

    def source(i, j):
        if i not in sources:
            own = field[i].astype(jnp.float32)
            other = jnp.zeros_like(own)
            if i < total_cols:
                other = unpack_border(halo[i // PACK].astype(jnp.float32), i % PACK, side)
            mixed = [own] * tiles
            mixed[0] = jnp.where(lane >= LANES - RMAX, other, own)
            mixed[-1] = jnp.where(lane < RMAX, other, own)
            sources[i] = mixed
        return sources[i][j]

    for i in places:
        for j in range(tiles):
            shift = (RMAX - TILE * j) % LANES
            first = pltpu.roll(source(i, j), shift, 1)
            second = pltpu.roll(source(i + 1, j), (shift + SPAN) % LANES, 1)
            windows[j, i] = jnp.where(lane < SPAN, first, second).astype(windows.dtype)


def annulus_body(frames, cols, radii, dop_far, mask_far, lag_far, sums, counts, series, lag_near, dop, mask_in, bands, weights,
                 field, halo, windows, wide, packs, packed16, halo_in, unpacked, natural, local_sem, send, recv):
    fetch_dop = pltpu.make_async_copy(dop_far, dop, local_sem.at[0])
    fetch_mask = pltpu.make_async_copy(mask_far, mask_in, local_sem.at[1])
    fetch_dop.start()
    fetch_mask.start()
    fetch_lags = pltpu.make_async_copy(lag_far, lag_near, local_sem.at[2])
    fetch_lags.start()
    count_s, count_t = lax.axis_size("space"), lax.axis_size("tm")
    s, t, side = lax.axis_index("space"), lax.axis_index("tm"), lax.axis_index("row")
    has_lo, has_hi = s > 0, s < count_s - 1
    has_pr, has_nx = t > 0, t < count_t - 1
    lo, hi = {"space": s - 1}, {"space": s + 1}
    lo_x, hi_x = {"space": s - 1, "row": 1 - side}, {"space": s + 1, "row": 1 - side}
    partner = {"row": 1 - side}
    prev, nxt = {"tm": t - 1}, {"tm": t + 1}
    groups = cols // PACK
    reach_groups = RMAX // PACK
    top = RMAX + cols
    sent = frames * cols
    always = None

    def when(cond, act):
        if cond is None:
            act()
        else:
            pl.when(cond)(act)

    barrier = pltpu.get_barrier_semaphore()

    def greet(*devices):
        def act():
            for device in devices:
                pl.semaphore_signal(barrier, inc=1, device_id=device, device_id_type=MESH)
        return act

    greet(partner)()
    pl.when(has_lo)(greet(lo, lo_x))
    pl.when(has_hi)(greet(hi, hi_x))
    pl.when(has_pr)(greet(prev))
    pl.when(has_nx)(greet(nxt))

    fetch_dop.wait()
    for c in range(cols):
        wide[REACH + c] = dop[pl.ds(c, frames, stride=cols), :]
    for g in range(groups):
        packs[g] = pack_borders([wide[REACH + g * PACK + k] for k in range(PACK)], side)

    def zero(ref, start, size):
        def act():
            ref[pl.ds(start, size)] = jnp.zeros((size,) + ref.shape[1:], ref.dtype)
        return act

    no_lo, no_hi, no_pr = s == 0, s == count_s - 1, t == 0
    field[pl.ds(top + RMAX, 1)] = jnp.zeros((1, frames, LANES), field.dtype)
    for cond, low in ((no_lo, True), (no_hi, False)):
        pl.when(cond)(zero(wide, 0 if low else REACH + cols, REACH))
        pl.when(cond)(zero(halo_in, 0 if low else groups + 1, 1))
        pl.when(cond)(zero(field, 0 if low else top, RMAX))
        pl.when(cond)(zero(halo, 0 if low else reach_groups + groups, reach_groups))
    pl.when(no_pr)(zero(series, 0, sent))

    def copy(index, source, target, device):
        return pltpu.make_async_remote_copy(
            src_ref=source, dst_ref=target, send_sem=send.at[index], recv_sem=recv.at[index],
            device_id=device, device_id_type=MESH,
        )

    first = [
        (copy(0, wide.at[pl.ds(REACH, REACH)], wide.at[pl.ds(REACH + cols, REACH)], lo), has_lo, has_hi),
        (copy(1, wide.at[pl.ds(cols, REACH)], wide.at[pl.ds(0, REACH)], hi), has_hi, has_lo),
        (copy(2, packs, halo_in.at[pl.ds(1, groups)], partner), always, always),
        (copy(3, packs.at[pl.ds(0, 1)], halo_in.at[pl.ds(groups + 1, 1)], lo_x), has_lo, has_hi),
        (copy(4, packs.at[pl.ds(groups - 1, 1)], halo_in.at[pl.ds(0, 1)], hi_x), has_hi, has_lo),
    ]
    second = [
        (copy(5, field.at[pl.ds(RMAX, RMAX)], field.at[pl.ds(top, RMAX)], lo), has_lo, has_hi),
        (copy(6, field.at[pl.ds(cols, RMAX)], field.at[pl.ds(0, RMAX)], hi), has_hi, has_lo),
        (copy(7, packed16, halo.at[pl.ds(reach_groups, groups)], partner), always, always),
        (copy(8, packed16.at[pl.ds(0, reach_groups)],
              halo.at[pl.ds(reach_groups + groups, reach_groups)], lo_x), has_lo, has_hi),
        (copy(9, packed16.at[pl.ds(groups - reach_groups, reach_groups)],
              halo.at[pl.ds(0, reach_groups)], hi_x), has_hi, has_lo),
        (copy(10, series.at[pl.ds(sent, sent)], series.at[pl.ds(0, sent)], nxt), has_nx, has_pr),
    ]

    met = lambda flag: jnp.where(flag, 1, 0).astype(jnp.int32)
    pl.semaphore_wait(barrier, 1 + 2 * met(has_lo) + 2 * met(has_hi) + met(has_pr) + met(has_nx))
    for moved, sends, _ in first:
        when(sends, moved.start)
    fetch_mask.wait()
    fetch_lags.wait()
    build_weights(radii, mask_in, bands, weights, counts)
    for moved, _, receives in first:
        when(receives, moved.wait_recv)

    for i in range(cols + 2 * REACH):
        place = i + PACK - REACH
        unpacked[i] = unpack_border(halo_in[place // PACK], place % PACK, side)
    lane = lane_iota((frames, LANES))
    for g in range(groups):
        smoothed = []
        for k in range(PACK):
            c = g * PACK + k
            own, other = [
                functools.reduce(lambda a, b: a + b, [gaussian_taps[i] * ref[c + i] for i in range(len(gaussian_taps))])
                for ref in (wide, unpacked)
            ]
            total = None
            for i, tap in enumerate(gaussian_taps):
                shift = i - REACH
                if shift > 0:
                    moved = pltpu.roll(jnp.where(lane < shift, other, own), LANES - shift, 1)
                elif shift < 0:
                    moved = pltpu.roll(jnp.where(lane >= LANES + shift, other, own), -shift, 1)
                else:
                    moved = own
                total = tap * moved if total is None else total + tap * moved
            smoothed.append(total)
            field[RMAX + c] = total.astype(field.dtype)
            natural[pl.ds(c, frames, stride=cols), :] = total
        packed16[g] = pack_borders(smoothed, side).astype(packed16.dtype)
    series[pl.ds(sent, sent)] = natural[...].astype(series.dtype)

    for moved, sends, _ in second:
        when(sends, moved.start)
    for moved, sends, _ in first:
        when(sends, moved.wait_send)
    second[2][0].wait_recv()
    build_windows(range(RMAX, top - 1), frames, top + RMAX, side, field, halo, windows)
    for moved, _, receives in second[:2] + second[3:5]:
        when(receives, moved.wait_recv)
    rest = list(range(RMAX)) + list(range(top - 1, top + RMAX))
    build_windows(rest, frames, top + RMAX, side, field, halo, windows)

    pairs = weights.shape[0] // LANES
    halves = sums.shape[1]
    for j in range(sums.shape[0]):
        left = jnp.concatenate(
            [windows[j, pl.ds(2 * g, cols)].reshape(cols * frames, LANES) for g in range(pairs)], axis=1
        )
        total = jnp.dot(left, weights[...], preferred_element_type=jnp.float32)
        for h in range(halves):
            sums[j, h] = total[:, h * LANES : (h + 1) * LANES]

    when(has_pr, second[5][0].wait_recv)
    for moved, sends, _ in second:
        when(sends, moved.wait_send)


def correlate_body(frames, cols, radii, lags, lag_far, counts, series, sums, out, lag_list, spread, parts, sem):
    fetch = pltpu.make_async_copy(lag_far, lag_list, sem)
    fetch.start()
    tiles = LANES // TILE
    f32 = jnp.float32
    rows = lax.broadcasted_iota(jnp.int32, (LANES, tiles * LANES), 0)
    places = lax.broadcasted_iota(jnp.int32, (LANES, tiles * LANES), 1)
    pick = jnp.where(rows == (places // LANES) * TILE + places % TILE, 1.0, 0.0).astype(jnp.bfloat16)
    spread[...] = jnp.dot(series[...], pick, preferred_element_type=f32)
    fetch.wait()

    halves = radii * TILE // LANES
    starts = [frames - lag_list[l] for l in range(lags)]
    for j in range(tiles):
        totals = [[None] * halves for _ in range(lags)]
        for t in range(frames):
            annulus = [sums[j, h, pl.ds(t, cols, stride=frames), :] for h in range(halves)]
            for l in range(lags):
                begin = pl.multiple_of((starts[l] + t) * cols, 8)
                earlier = spread[pl.ds(begin, cols), pl.ds(j * LANES, LANES)]
                for h in range(halves):
                    term = earlier * annulus[h]
                    totals[l][h] = term if t == 0 else totals[l][h] + term
        for l in range(lags):
            for h in range(halves):
                parts[j, l, h] = totals[l][h]

    group = lane_iota((cols, LANES)) // TILE
    for r in range(radii):
        h, rr = r // PACK, r % PACK
        count = counts[r : r + 1, 0:1]
        for l in range(lags):
            whole = None
            for j in range(tiles):
                shift = (TILE * (j - rr)) % LANES
                piece = parts[j, l, h]
                piece = pltpu.roll(piece, shift, 1) if shift else piece
                whole = piece if whole is None else jnp.where(group == j, piece, whole)
            out[r, l] = whole / count


def local(doppler, cycle_masks, lag_list):
    frames, cols, rows = doppler.shape
    radii, side = cycle_masks.shape[:2]
    lags = lag_list.shape[0]
    assert rows == LANES and frames == RMAX and side == 2 * RMAX + 1 and cols % 8 == 0 and cols >= RMAX
    assert lax.axis_size("row") == 2 and radii % 8 == 0 and radii * TILE % LANES == 0
    groups = cols // PACK
    ext = cols + 2 * RMAX
    tiles, halves = LANES // TILE, radii * TILE // LANES
    pairs = (side + 1) // 2
    f32, bf16 = jnp.float32, jnp.bfloat16
    vmem = pl.BlockSpec(memory_space=pltpu.VMEM)
    far = pl.BlockSpec(memory_space=pltpu.HBM)
    sums, counts, series, lag_near = pl.pallas_call(
        functools.partial(annulus_body, frames, cols, radii),
        out_shape=(
            jax.ShapeDtypeStruct((tiles, halves, cols * frames, LANES), f32),
            jax.ShapeDtypeStruct((radii, LANES), f32),
            jax.ShapeDtypeStruct((2 * frames * cols, LANES), bf16),
            jax.ShapeDtypeStruct((lags,), jnp.int32),
        ),
        in_specs=[far, far, far],
        out_specs=(vmem, vmem, vmem, vmem),
        scratch_shapes=[
            pltpu.VMEM((frames * cols, LANES), f32),
            pltpu.VMEM((side, radii, side), jnp.int32),
            pltpu.VMEM((pairs, radii * TILE, LANES), f32),
            pltpu.VMEM((pairs * LANES, radii * TILE), bf16),
            pltpu.VMEM((ext + 1, frames, LANES), bf16),
            pltpu.VMEM((ext // PACK, frames, LANES), bf16),
            pltpu.VMEM((tiles, ext, frames, LANES), bf16),
            pltpu.VMEM((cols + 2 * REACH, frames, LANES), f32),
            pltpu.VMEM((groups, frames, LANES), f32),
            pltpu.VMEM((groups, frames, LANES), bf16),
            pltpu.VMEM((groups + 2, frames, LANES), f32),
            pltpu.VMEM((cols + 2 * REACH, frames, LANES), f32),
            pltpu.VMEM((frames * cols, LANES), f32),
            pltpu.SemaphoreType.DMA((3,)),
            pltpu.SemaphoreType.DMA((11,)),
            pltpu.SemaphoreType.DMA((11,)),
        ],
        compiler_params=pltpu.CompilerParams(
            collective_id=0, has_side_effects=True, vmem_limit_bytes=VMEM_SHARE
        ),
    )(doppler.reshape(frames * cols, LANES), jnp.transpose(cycle_masks, (1, 0, 2)), lag_list)
    out = pl.pallas_call(
        functools.partial(correlate_body, frames, cols, radii, lags),
        out_shape=jax.ShapeDtypeStruct((radii, lags, cols, LANES), f32),
        in_specs=[vmem, vmem, vmem, vmem],
        out_specs=vmem,
        scratch_shapes=[
            pltpu.SMEM((lags,), jnp.int32),
            pltpu.VMEM((2 * frames * cols, tiles * LANES), f32),
            pltpu.VMEM((tiles, lags, halves, cols, LANES), f32),
            pltpu.SemaphoreType.DMA,
        ],
        compiler_params=pltpu.CompilerParams(vmem_limit_bytes=24 * 2**20),
    )(lag_near, counts, series, sums)
    return out[None]


def solution(mesh):
    return jax.shard_map(
        local,
        mesh=mesh,
        in_specs=(P("tm", ("patch", "space"), "row"), P(), P()),
        out_specs=P("tm", None, None, ("patch", "space"), "row"),
        check_vma=False,
    )
```

```python
import functools

import jax
import jax.numpy as jnp
from jax import lax
from jax.experimental import pallas as pl
from jax.experimental.pallas import tpu as pltpu
from jax.sharding import PartitionSpec as P

MESH = pl.DeviceIdType.MESH
RMAX = 16
LANES = 128
TILE = 32
SPAN = 2 * TILE
PACK = LANES // TILE
gaussian_taps = (0.05448868, 0.24420134, 0.40261995, 0.24420134, 0.05448868)
REACH = len(gaussian_taps) // 2
VMEM_SHARE = 60 * 2**20


def lane_iota(shape):
    return lax.broadcasted_iota(jnp.int32, shape, len(shape) - 1)


def pack_borders(blocks, side):
    group = lane_iota(blocks[0].shape) // TILE
    base = (1 - side) * TILE
    packed = None
    for k, block in enumerate(blocks):
        turned = pltpu.roll(block, lax.rem(k * TILE + base, LANES), 1)
        packed = turned if packed is None else jnp.where(group == k, turned, packed)
    return packed


def unpack_border(packed, k, side):
    base = side * (LANES - TILE)
    turned = pltpu.roll(packed, lax.rem(LANES - k * TILE + base, LANES), 1)
    lane = lane_iota(packed.shape)
    return jnp.where((lane >= base) & (lane < base + TILE), turned, jnp.zeros_like(turned))


def build_weights(radii, mask_in, bands, weights, counts, early):
    side = mask_in.shape[0]
    pairs = weights.shape[0] // LANES
    bits = mask_in[...].astype(jnp.float32).reshape(side * radii, side).astype(jnp.bfloat16)
    rows = lax.broadcasted_iota(jnp.int32, (side, LANES), 0)
    lane = lane_iota((side, LANES))
    put = [jnp.where(lane == rows + k * SPAN, 1.0, 0.0).astype(jnp.bfloat16) for k in range(2)]
    even, odd = [jnp.dot(bits, p, preferred_element_type=jnp.float32) for p in put]
    pieces = []
    for g in range(pairs):
        a = 2 * g
        piece = even[a * radii : (a + 1) * radii]
        if a + 1 < side:
            piece = piece + odd[(a + 1) * radii : (a + 2) * radii]
        pieces.append(piece)
    total = functools.reduce(lambda x, y: x + y, pieces)
    counts[...] = jnp.broadcast_to(jnp.sum(total, axis=1, keepdims=True), counts.shape)

    def build(some):
        for g in some:
            for q in range(TILE):
                bands[g, pl.ds(q, radii, stride=TILE), :] = pltpu.roll(pieces[g], q, 1) if q else pieces[g]
            weights[pl.ds(g * LANES, LANES), :] = bands[g].T.astype(weights.dtype)

    build(range(early))
    return lambda: build(range(early, pairs))


def build_windows(places, frames, total_cols, side, field, halo, windows):
    lane = lane_iota((frames, LANES))
    tiles = windows.shape[0]
    sources = {}

    def source(i, j):
        if i not in sources:
            own = field[i].astype(jnp.float32)
            other = jnp.zeros_like(own)
            if i < total_cols:
                other = unpack_border(halo[i // PACK].astype(jnp.float32), i % PACK, side)
            mixed = [own] * tiles
            mixed[0] = jnp.where(lane >= LANES - RMAX, other, own)
            mixed[-1] = jnp.where(lane < RMAX, other, own)
            sources[i] = mixed
        return sources[i][j]

    for i in places:
        for j in range(tiles):
            shift = (RMAX - TILE * j) % LANES
            first = pltpu.roll(source(i, j), shift, 1)
            second = pltpu.roll(source(i + 1, j), (shift + SPAN) % LANES, 1)
            windows[j, i] = jnp.where(lane < SPAN, first, second).astype(windows.dtype)


def body(frames, cols, radii, lags, dop_far, mask_far, lag_far, out_far, sums, counts, series, lag_list, spread, parts,
         out, dop, mask_in, bands, weights, field, halo, windows, wide, packs, packed16, halo_in, unpacked, natural,
         local_sem, out_sem, send, recv):
    fetch_dop = pltpu.make_async_copy(dop_far, dop, local_sem.at[0])
    fetch_mask = pltpu.make_async_copy(mask_far, mask_in, local_sem.at[1])
    fetch_dop.start()
    fetch_mask.start()
    fetch_lags = pltpu.make_async_copy(lag_far, lag_list, local_sem.at[2])
    fetch_lags.start()
    count_s, count_t = lax.axis_size("space"), lax.axis_size("tm")
    s, t, side = lax.axis_index("space"), lax.axis_index("tm"), lax.axis_index("row")
    has_lo, has_hi = s > 0, s < count_s - 1
    has_pr, has_nx = t > 0, t < count_t - 1
    lo, hi = {"space": s - 1}, {"space": s + 1}
    lo_x, hi_x = {"space": s - 1, "row": 1 - side}, {"space": s + 1, "row": 1 - side}
    partner = {"row": 1 - side}
    prev, nxt = {"tm": t - 1}, {"tm": t + 1}
    groups = cols // PACK
    reach_groups = RMAX // PACK
    top = RMAX + cols
    sent = frames * cols
    always = None

    def when(cond, act):
        if cond is None:
            act()
        else:
            pl.when(cond)(act)

    barrier = pltpu.get_barrier_semaphore()

    def greet(*devices):
        def act():
            for device in devices:
                pl.semaphore_signal(barrier, inc=1, device_id=device, device_id_type=MESH)
        return act

    greet(partner)()
    pl.when(has_lo)(greet(lo, lo_x))
    pl.when(has_hi)(greet(hi, hi_x))
    pl.when(has_pr)(greet(prev))
    pl.when(has_nx)(greet(nxt))

    fetch_dop.wait()
    for c in range(cols):
        wide[REACH + c] = dop[pl.ds(c, frames, stride=cols), :]
    for g in range(groups):
        packs[g] = pack_borders([wide[REACH + g * PACK + k] for k in range(PACK)], side)

    def zero(ref, start, size):
        def act():
            ref[pl.ds(start, size)] = jnp.zeros((size,) + ref.shape[1:], ref.dtype)
        return act

    no_lo, no_hi, no_pr = s == 0, s == count_s - 1, t == 0
    field[pl.ds(top + RMAX, 1)] = jnp.zeros((1, frames, LANES), field.dtype)
    for cond, low in ((no_lo, True), (no_hi, False)):
        pl.when(cond)(zero(wide, 0 if low else REACH + cols, REACH))
        pl.when(cond)(zero(halo_in, 0 if low else groups + 1, 1))
        pl.when(cond)(zero(field, 0 if low else top, RMAX))
        pl.when(cond)(zero(halo, 0 if low else reach_groups + groups, reach_groups))
    pl.when(no_pr)(zero(series, 0, sent))

    def copy(index, source, target, device):
        return pltpu.make_async_remote_copy(
            src_ref=source, dst_ref=target, send_sem=send.at[index], recv_sem=recv.at[index],
            device_id=device, device_id_type=MESH,
        )

    first = [
        (copy(0, wide.at[pl.ds(REACH, REACH)], wide.at[pl.ds(REACH + cols, REACH)], lo), has_lo, has_hi),
        (copy(1, wide.at[pl.ds(cols, REACH)], wide.at[pl.ds(0, REACH)], hi), has_hi, has_lo),
        (copy(2, packs, halo_in.at[pl.ds(1, groups)], partner), always, always),
        (copy(3, packs.at[pl.ds(0, 1)], halo_in.at[pl.ds(groups + 1, 1)], lo_x), has_lo, has_hi),
        (copy(4, packs.at[pl.ds(groups - 1, 1)], halo_in.at[pl.ds(0, 1)], hi_x), has_hi, has_lo),
    ]
    second = [
        (copy(5, field.at[pl.ds(RMAX, RMAX)], field.at[pl.ds(top, RMAX)], lo), has_lo, has_hi),
        (copy(6, field.at[pl.ds(cols, RMAX)], field.at[pl.ds(0, RMAX)], hi), has_hi, has_lo),
        (copy(7, packed16, halo.at[pl.ds(reach_groups, groups)], partner), always, always),
        (copy(8, packed16.at[pl.ds(0, reach_groups)],
              halo.at[pl.ds(reach_groups + groups, reach_groups)], lo_x), has_lo, has_hi),
        (copy(9, packed16.at[pl.ds(groups - reach_groups, reach_groups)],
              halo.at[pl.ds(0, reach_groups)], hi_x), has_hi, has_lo),
        (copy(10, series.at[pl.ds(sent, sent)], series.at[pl.ds(0, sent)], nxt), has_nx, has_pr),
    ]

    def spread_frames(start):
        size = LANES // TILE * LANES
        rows = lax.broadcasted_iota(jnp.int32, (LANES, size), 0)
        places = lax.broadcasted_iota(jnp.int32, (LANES, size), 1)
        pick = jnp.where(rows == (places // LANES) * TILE + places % TILE, 1.0, 0.0).astype(series.dtype)
        chosen = jnp.dot(series[pl.ds(start, frames * cols)], pick, preferred_element_type=jnp.float32)
        spread[pl.ds(start // cols, frames)] = chosen.reshape(frames, cols, size)

    met = lambda flag: jnp.where(flag, 1, 0).astype(jnp.int32)
    pl.semaphore_wait(barrier, 1 + 2 * met(has_lo) + 2 * met(has_hi) + met(has_pr) + met(has_nx))
    for moved, sends, _ in first:
        when(sends, moved.start)
    fetch_mask.wait()
    fetch_lags.wait()
    pairs = weights.shape[0] // LANES
    finish_weights = build_weights(radii, mask_in, bands, weights, counts, pairs // 3)
    for moved, _, receives in first:
        when(receives, moved.wait_recv)

    for i in range(cols + 2 * REACH):
        place = i + PACK - REACH
        unpacked[i] = unpack_border(halo_in[place // PACK], place % PACK, side)
    lane = lane_iota((frames, LANES))
    for g in range(groups):
        smoothed = []
        for k in range(PACK):
            c = g * PACK + k
            own, other = [
                functools.reduce(lambda a, b: a + b, [gaussian_taps[i] * ref[c + i] for i in range(len(gaussian_taps))])
                for ref in (wide, unpacked)
            ]
            total = None
            for i, tap in enumerate(gaussian_taps):
                shift = i - REACH
                if shift > 0:
                    moved = pltpu.roll(jnp.where(lane < shift, other, own), LANES - shift, 1)
                elif shift < 0:
                    moved = pltpu.roll(jnp.where(lane >= LANES + shift, other, own), -shift, 1)
                else:
                    moved = own
                total = tap * moved if total is None else total + tap * moved
            smoothed.append(total)
            field[RMAX + c] = total.astype(field.dtype)
            natural[pl.ds(c, frames, stride=cols), :] = total
        packed16[g] = pack_borders(smoothed, side).astype(packed16.dtype)
    series[pl.ds(sent, sent)] = natural[...].astype(series.dtype)

    for moved, sends, _ in second:
        when(sends, moved.start)
    spread_frames(frames * cols)
    finish_weights()
    for moved, sends, _ in first:
        when(sends, moved.wait_send)
    second[2][0].wait_recv()
    build_windows(range(RMAX, top - 1), frames, top + RMAX, side, field, halo, windows)

    tiles, halves = sums.shape[:2]
    block = 8
    rows = block * frames

    def products(start, chosen):
        left = jnp.concatenate(
            [
                jnp.concatenate(
                    [windows[j, pl.ds(start + 2 * g, block)].reshape(rows, LANES) for g in chosen], axis=1
                )
                for j in range(tiles)
            ],
            axis=0,
        )
        right = jnp.concatenate([weights[pl.ds(g * LANES, LANES), :] for g in chosen], axis=0)
        return jnp.dot(left, right, preferred_element_type=jnp.float32)

    def inside(start, g):
        return start + 2 * g >= RMAX and start + 2 * g + block <= top - 1

    for own in (True, False):
        for start in range(0, cols, block):
            total = products(start, [g for g in range(pairs) if inside(start, g) == own])
            for j in range(tiles):
                for h in range(halves):
                    piece = total[j * rows : (j + 1) * rows, h * LANES : (h + 1) * LANES]
                    place = pl.ds(start * frames, rows)
                    sums[j, h, place, :] = piece if own else sums[j, h, place, :] + piece
        if own:
            for moved, _, receives in second[:2] + second[3:5]:
                when(receives, moved.wait_recv)
            rest = list(range(RMAX)) + list(range(top - 1, top + RMAX))
            build_windows(rest, frames, top + RMAX, side, field, halo, windows)

    when(has_pr, second[5][0].wait_recv)
    spread_frames(0)
    correlate(frames, cols, radii, lags, lag_list, counts, sums, spread, parts, out, out_far, out_sem)
    for moved, sends, _ in second:
        when(sends, moved.wait_send)


def correlate(frames, cols, radii, lags, lag_list, counts, sums, spread, parts, out, out_far, out_sem):
    tiles = LANES // TILE
    halves = radii * TILE // LANES
    starts = [frames - lag_list[l] for l in range(lags)]
    for j in range(tiles):
        totals = [[None] * halves for _ in range(lags)]
        for t in range(frames):
            annulus = [sums[j, h, pl.ds(t, cols, stride=frames), :] for h in range(halves)]
            for l in range(lags):
                earlier = spread[starts[l] + t, :, j * LANES : (j + 1) * LANES]
                for h in range(halves):
                    term = earlier * annulus[h]
                    totals[l][h] = term if t == 0 else totals[l][h] + term
        for l in range(lags):
            for h in range(halves):
                parts[j, l, h] = totals[l][h]

    group = lane_iota((cols, LANES)) // TILE
    for r in range(radii):
        h, rr = r // PACK, r % PACK
        count = counts[r : r + 1, 0:1]
        for l in range(lags):
            whole = None
            for j in range(tiles):
                shift = (TILE * (j - rr)) % LANES
                piece = parts[j, l, h]
                piece = pltpu.roll(piece, shift, 1) if shift else piece
                whole = piece if whole is None else jnp.where(group == j, piece, whole)
            out[r, l] = whole / count
        pltpu.make_async_copy(out.at[r], out_far.at[r], out_sem.at[r]).start()
    for r in range(radii):
        pltpu.make_async_copy(out.at[r], out_far.at[r], out_sem.at[r]).wait()


def local(doppler, cycle_masks, lag_list):
    frames, cols, rows = doppler.shape
    radii, side = cycle_masks.shape[:2]
    lags = lag_list.shape[0]
    assert rows == LANES and frames == RMAX and side == 2 * RMAX + 1 and cols % 8 == 0 and cols >= RMAX
    assert lax.axis_size("row") == 2 and radii % 8 == 0 and radii * TILE % LANES == 0
    groups = cols // PACK
    ext = cols + 2 * RMAX
    tiles, halves = LANES // TILE, radii * TILE // LANES
    pairs = (side + 1) // 2
    f32, bf16 = jnp.float32, jnp.bfloat16
    vmem = pl.BlockSpec(memory_space=pltpu.VMEM)
    far = pl.BlockSpec(memory_space=pltpu.HBM)
    out = pl.pallas_call(
        functools.partial(body, frames, cols, radii, lags),
        out_shape=jax.ShapeDtypeStruct((radii, lags, cols, LANES), f32),
        in_specs=[far, far, far],
        out_specs=far,
        scratch_shapes=[
            pltpu.VMEM((tiles, halves, cols * frames, LANES), f32),
            pltpu.VMEM((radii, LANES), f32),
            pltpu.VMEM((2 * frames * cols, LANES), bf16),
            pltpu.SMEM((lags,), jnp.int32),
            pltpu.VMEM((2 * frames, cols, tiles * LANES), f32),
            pltpu.VMEM((tiles, lags, halves, cols, LANES), f32),
            pltpu.VMEM((radii, lags, cols, LANES), f32),
            pltpu.VMEM((frames * cols, LANES), f32),
            pltpu.VMEM((side, radii, side), jnp.int32),
            pltpu.VMEM((pairs, radii * TILE, LANES), f32),
            pltpu.VMEM((pairs * LANES, radii * TILE), bf16),
            pltpu.VMEM((ext + 1, frames, LANES), bf16),
            pltpu.VMEM((ext // PACK, frames, LANES), bf16),
            pltpu.VMEM((tiles, ext, frames, LANES), bf16),
            pltpu.VMEM((cols + 2 * REACH, frames, LANES), f32),
            pltpu.VMEM((groups, frames, LANES), f32),
            pltpu.VMEM((groups, frames, LANES), bf16),
            pltpu.VMEM((groups + 2, frames, LANES), f32),
            pltpu.VMEM((cols + 2 * REACH, frames, LANES), f32),
            pltpu.VMEM((frames * cols, LANES), f32),
            pltpu.SemaphoreType.DMA((3,)),
            pltpu.SemaphoreType.DMA((radii,)),
            pltpu.SemaphoreType.DMA((11,)),
            pltpu.SemaphoreType.DMA((11,)),
        ],
        compiler_params=pltpu.CompilerParams(
            collective_id=0, has_side_effects=True, vmem_limit_bytes=VMEM_SHARE
        ),
    )(doppler.reshape(frames * cols, LANES), jnp.transpose(cycle_masks, (1, 0, 2)), lag_list)
    return out[None]


def solution(mesh):
    return jax.shard_map(
        local,
        mesh=mesh,
        in_specs=(P("tm", ("patch", "space"), "row"), P(), P()),
        out_specs=P("tm", None, None, ("patch", "space"), "row"),
        check_vma=False,
    )
```

```python
import functools

import jax
import jax.numpy as jnp
from jax import lax
from jax.experimental import pallas as pl
from jax.experimental.pallas import tpu as pltpu
from jax.sharding import PartitionSpec as P

MESH = pl.DeviceIdType.MESH
RMAX = 16
LANES = 128
TILE = 32
SPAN = 2 * TILE
PACK = LANES // TILE
gaussian_taps = (0.05448868, 0.24420134, 0.40261995, 0.24420134, 0.05448868)
REACH = len(gaussian_taps) // 2
VMEM_SHARE = 60 * 2**20


def lane_iota(shape):
    return lax.broadcasted_iota(jnp.int32, shape, len(shape) - 1)


def pack_borders(blocks, side):
    group = lane_iota(blocks[0].shape) // TILE
    base = (1 - side) * TILE
    packed = None
    for k, block in enumerate(blocks):
        turned = pltpu.roll(block, lax.rem(k * TILE + base, LANES), 1)
        packed = turned if packed is None else jnp.where(group == k, turned, packed)
    return packed


def unpack_border(packed, k, side):
    base = side * (LANES - TILE)
    turned = pltpu.roll(packed, lax.rem(LANES - k * TILE + base, LANES), 1)
    lane = lane_iota(packed.shape)
    return jnp.where((lane >= base) & (lane < base + TILE), turned, jnp.zeros_like(turned))


def build_weights(radii, mask_in, bands, weights, counts, early):
    side = mask_in.shape[0]
    pairs = weights.shape[1] // LANES
    bits = mask_in[...].astype(jnp.float32).reshape(side * radii, side).astype(jnp.bfloat16)
    rows = lax.broadcasted_iota(jnp.int32, (side, LANES), 0)
    lane = lane_iota((side, LANES))
    put = [jnp.where(lane == rows + k * SPAN, 1.0, 0.0).astype(jnp.bfloat16) for k in range(2)]
    even, odd = [jnp.dot(bits, p, preferred_element_type=jnp.float32) for p in put]
    pieces = []
    for g in range(pairs):
        a = 2 * g
        piece = even[a * radii : (a + 1) * radii]
        if a + 1 < side:
            piece = piece + odd[(a + 1) * radii : (a + 2) * radii]
        pieces.append(piece)
    total = functools.reduce(lambda x, y: x + y, pieces)
    counts[...] = jnp.broadcast_to(jnp.sum(total, axis=1, keepdims=True), counts.shape)

    def build(some):
        for g in some:
            for q in range(TILE):
                bands[g, pl.ds(q, radii, stride=TILE), :] = pltpu.roll(pieces[g], q, 1) if q else pieces[g]
            weights[:, pl.ds(g * LANES, LANES)] = bands[g].astype(weights.dtype)

    build(range(early))
    return lambda: build(range(early, pairs))


def build_windows(places, frames, total_cols, side, field, halo, windows):
    lane = lane_iota((frames, LANES))
    tiles = windows.shape[0]
    sources = {}

    def source(i, j):
        if i not in sources:
            own = field[i].astype(jnp.float32)
            other = jnp.zeros_like(own)
            if i < total_cols:
                other = unpack_border(halo[i // PACK].astype(jnp.float32), i % PACK, side)
            mixed = [own] * tiles
            mixed[0] = jnp.where(lane >= LANES - RMAX, other, own)
            mixed[-1] = jnp.where(lane < RMAX, other, own)
            sources[i] = mixed
        return sources[i][j]

    for i in places:
        for j in range(tiles):
            shift = (RMAX - TILE * j) % LANES
            first = pltpu.roll(source(i, j), shift, 1)
            second = pltpu.roll(source(i + 1, j), (shift + SPAN) % LANES, 1)
            windows[j, i] = jnp.where(lane < SPAN, first, second).astype(windows.dtype)


def body(frames, cols, radii, lags, dop_far, mask_far, lag_far, out_far, counts, sums, series, lag_list, spread, parts,
         out, dop, mask_in, bands, weights, field, halo, windows, wide, packs, packed16, halo_in, unpacked, natural,
         local_sem, out_sem, send, recv):
    fetch_dop = pltpu.make_async_copy(dop_far, dop, local_sem.at[0])
    fetch_mask = pltpu.make_async_copy(mask_far, mask_in, local_sem.at[1])
    fetch_dop.start()
    fetch_mask.start()
    fetch_lags = pltpu.make_async_copy(lag_far, lag_list, local_sem.at[2])
    fetch_lags.start()
    count_s, count_t = lax.axis_size("space"), lax.axis_size("tm")
    s, t, side = lax.axis_index("space"), lax.axis_index("tm"), lax.axis_index("row")
    has_lo, has_hi = s > 0, s < count_s - 1
    has_pr, has_nx = t > 0, t < count_t - 1
    lo, hi = {"space": s - 1}, {"space": s + 1}
    lo_x, hi_x = {"space": s - 1, "row": 1 - side}, {"space": s + 1, "row": 1 - side}
    partner = {"row": 1 - side}
    prev, nxt = {"tm": t - 1}, {"tm": t + 1}
    groups = cols // PACK
    reach_groups = RMAX // PACK
    top = RMAX + cols
    sent = frames * cols
    always = None

    def when(cond, act):
        if cond is None:
            act()
        else:
            pl.when(cond)(act)

    barrier = pltpu.get_barrier_semaphore()

    def greet(*devices):
        def act():
            for device in devices:
                pl.semaphore_signal(barrier, inc=1, device_id=device, device_id_type=MESH)
        return act

    greet(partner)()
    pl.when(has_lo)(greet(lo, lo_x))
    pl.when(has_hi)(greet(hi, hi_x))
    pl.when(has_pr)(greet(prev))
    pl.when(has_nx)(greet(nxt))

    fetch_dop.wait()
    for c in range(cols):
        wide[REACH + c] = dop[pl.ds(c, frames, stride=cols), :]
    for g in range(groups):
        packs[g] = pack_borders([wide[REACH + g * PACK + k] for k in range(PACK)], side)

    def zero(ref, start, size):
        def act():
            ref[pl.ds(start, size)] = jnp.zeros((size,) + ref.shape[1:], ref.dtype)
        return act

    no_lo, no_hi, no_pr = s == 0, s == count_s - 1, t == 0
    field[pl.ds(top + RMAX, 1)] = jnp.zeros((1, frames, LANES), field.dtype)
    for cond, low in ((no_lo, True), (no_hi, False)):
        pl.when(cond)(zero(wide, 0 if low else REACH + cols, REACH))
        pl.when(cond)(zero(halo_in, 0 if low else groups + 1, 1))
        pl.when(cond)(zero(field, 0 if low else top, RMAX))
        pl.when(cond)(zero(halo, 0 if low else reach_groups + groups, reach_groups))
    pl.when(no_pr)(zero(series, 0, sent))

    def copy(index, source, target, device):
        return pltpu.make_async_remote_copy(
            src_ref=source, dst_ref=target, send_sem=send.at[index], recv_sem=recv.at[index],
            device_id=device, device_id_type=MESH,
        )

    first = [
        (copy(0, wide.at[pl.ds(REACH, REACH)], wide.at[pl.ds(REACH + cols, REACH)], lo), has_lo, has_hi),
        (copy(1, wide.at[pl.ds(cols, REACH)], wide.at[pl.ds(0, REACH)], hi), has_hi, has_lo),
        (copy(2, packs, halo_in.at[pl.ds(1, groups)], partner), always, always),
        (copy(3, packs.at[pl.ds(0, 1)], halo_in.at[pl.ds(groups + 1, 1)], lo_x), has_lo, has_hi),
        (copy(4, packs.at[pl.ds(groups - 1, 1)], halo_in.at[pl.ds(0, 1)], hi_x), has_hi, has_lo),
    ]
    second = [
        (copy(5, field.at[pl.ds(RMAX, RMAX)], field.at[pl.ds(top, RMAX)], lo), has_lo, has_hi),
        (copy(6, field.at[pl.ds(cols, RMAX)], field.at[pl.ds(0, RMAX)], hi), has_hi, has_lo),
        (copy(7, packed16, halo.at[pl.ds(reach_groups, groups)], partner), always, always),
        (copy(8, packed16.at[pl.ds(0, reach_groups)],
              halo.at[pl.ds(reach_groups + groups, reach_groups)], lo_x), has_lo, has_hi),
        (copy(9, packed16.at[pl.ds(groups - reach_groups, reach_groups)],
              halo.at[pl.ds(0, reach_groups)], hi_x), has_hi, has_lo),
        (copy(10, series.at[pl.ds(sent, sent)], series.at[pl.ds(0, sent)], nxt), has_nx, has_pr),
    ]

    def spread_frames(start):
        size = LANES // TILE * LANES
        rows = lax.broadcasted_iota(jnp.int32, (LANES, size), 0)
        places = lax.broadcasted_iota(jnp.int32, (LANES, size), 1)
        pick = jnp.where(rows == (places // LANES) * TILE + places % TILE, 1.0, 0.0).astype(series.dtype)
        chosen = jnp.dot(series[pl.ds(start, frames * cols)], pick, preferred_element_type=jnp.float32)
        spread[pl.ds(start // cols, frames)] = chosen.reshape(frames, cols, size)

    met = lambda flag: jnp.where(flag, 1, 0).astype(jnp.int32)
    pl.semaphore_wait(barrier, 1 + 2 * met(has_lo) + 2 * met(has_hi) + met(has_pr) + met(has_nx))
    for moved, sends, _ in first:
        when(sends, moved.start)
    fetch_mask.wait()
    fetch_lags.wait()
    pairs = weights.shape[1] // LANES
    finish_weights = build_weights(radii, mask_in, bands, weights, counts, pairs // 3)
    for moved, _, receives in first:
        when(receives, moved.wait_recv)

    for i in range(cols + 2 * REACH):
        place = i + PACK - REACH
        unpacked[i] = unpack_border(halo_in[place // PACK], place % PACK, side)
    lane = lane_iota((frames, LANES))
    for g in range(groups):
        smoothed = []
        for k in range(PACK):
            c = g * PACK + k
            own, other = [
                functools.reduce(lambda a, b: a + b, [gaussian_taps[i] * ref[c + i] for i in range(len(gaussian_taps))])
                for ref in (wide, unpacked)
            ]
            total = None
            for i, tap in enumerate(gaussian_taps):
                shift = i - REACH
                if shift > 0:
                    moved = pltpu.roll(jnp.where(lane < shift, other, own), LANES - shift, 1)
                elif shift < 0:
                    moved = pltpu.roll(jnp.where(lane >= LANES + shift, other, own), -shift, 1)
                else:
                    moved = own
                total = tap * moved if total is None else total + tap * moved
            smoothed.append(total)
            field[RMAX + c] = total.astype(field.dtype)
            natural[pl.ds(c, frames, stride=cols), :] = total
        packed16[g] = pack_borders(smoothed, side).astype(packed16.dtype)
    series[pl.ds(sent, sent)] = natural[...].astype(series.dtype)

    for moved, sends, _ in second:
        when(sends, moved.start)
    spread_frames(frames * cols)
    finish_weights()
    for moved, sends, _ in first:
        when(sends, moved.wait_send)
    second[2][0].wait_recv()
    build_windows(range(RMAX, top - 1), frames, top + RMAX, side, field, halo, windows)

    tiles, halves = sums.shape[:2]
    block = 8
    rows = block * frames

    def products(start, chosen):
        left = jnp.concatenate(
            [
                jnp.concatenate(
                    [windows[j, pl.ds(start + 2 * g, block)].reshape(rows, LANES) for g in chosen], axis=1
                )
                for j in range(tiles)
            ],
            axis=0,
        )
        right = jnp.concatenate([weights[:, pl.ds(g * LANES, LANES)] for g in chosen], axis=1)
        return lax.dot_general(left, right, (((1,), (1,)), ((), ())), preferred_element_type=jnp.float32)

    def inside(start, g):
        return start + 2 * g >= RMAX and start + 2 * g + block <= top - 1

    for own in (True, False):
        for start in range(0, cols, block):
            total = products(start, [g for g in range(pairs) if inside(start, g) == own])
            for j in range(tiles):
                for h in range(halves):
                    piece = total[j * rows : (j + 1) * rows, h * LANES : (h + 1) * LANES]
                    place = pl.ds(start * frames, rows)
                    sums[j, h, place, :] = piece if own else sums[j, h, place, :] + piece
        if own:
            for moved, _, receives in second[:2] + second[3:5]:
                when(receives, moved.wait_recv)
            rest = list(range(RMAX)) + list(range(top - 1, top + RMAX))
            build_windows(rest, frames, top + RMAX, side, field, halo, windows)

    when(has_pr, second[5][0].wait_recv)
    spread_frames(0)
    correlate(frames, cols, radii, lags, lag_list, sums, spread, parts, out, out_far, out_sem)
    for moved, sends, _ in second:
        when(sends, moved.wait_send)


def correlate(frames, cols, radii, lags, lag_list, sums, spread, parts, out, out_far, out_sem):
    tiles = LANES // TILE
    halves = radii * TILE // LANES
    starts = [frames - lag_list[l] for l in range(lags)]
    for j in range(tiles):
        totals = [[None] * halves for _ in range(lags)]
        for t in range(frames):
            annulus = [sums[j, h, pl.ds(t, cols, stride=frames), :] for h in range(halves)]
            for l in range(lags):
                earlier = spread[starts[l] + t, :, j * LANES : (j + 1) * LANES]
                for h in range(halves):
                    term = earlier * annulus[h]
                    totals[l][h] = term if t == 0 else totals[l][h] + term
        for l in range(lags):
            for h in range(halves):
                parts[j, l, h] = totals[l][h]

    group = lane_iota((cols, LANES)) // TILE
    for r in range(radii):
        h, rr = r // PACK, r % PACK
        for l in range(lags):
            whole = None
            for j in range(tiles):
                shift = (TILE * (j - rr)) % LANES
                piece = parts[j, l, h]
                piece = pltpu.roll(piece, shift, 1) if shift else piece
                whole = piece if whole is None else jnp.where(group == j, piece, whole)
            out[r, l] = whole
        pltpu.make_async_copy(out.at[r], out_far.at[r], out_sem.at[r]).start()
    for r in range(radii):
        pltpu.make_async_copy(out.at[r], out_far.at[r], out_sem.at[r]).wait()


def local(doppler, cycle_masks, lag_list):
    frames, cols, rows = doppler.shape
    radii, side = cycle_masks.shape[:2]
    lags = lag_list.shape[0]
    assert rows == LANES and frames == RMAX and side == 2 * RMAX + 1 and cols % 8 == 0 and cols >= RMAX
    assert lax.axis_size("row") == 2 and radii % 8 == 0 and radii * TILE % LANES == 0
    groups = cols // PACK
    ext = cols + 2 * RMAX
    tiles, halves = LANES // TILE, radii * TILE // LANES
    pairs = (side + 1) // 2
    f32, bf16 = jnp.float32, jnp.bfloat16
    far = pl.BlockSpec(memory_space=pltpu.HBM)
    out, counts = pl.pallas_call(
        functools.partial(body, frames, cols, radii, lags),
        out_shape=(
            jax.ShapeDtypeStruct((radii, lags, cols, LANES), f32),
            jax.ShapeDtypeStruct((radii, LANES), f32),
        ),
        in_specs=[far, far, far],
        out_specs=(far, pl.BlockSpec(memory_space=pltpu.VMEM)),
        scratch_shapes=[
            pltpu.VMEM((tiles, halves, cols * frames, LANES), f32),
            pltpu.VMEM((2 * frames * cols, LANES), bf16),
            pltpu.SMEM((lags,), jnp.int32),
            pltpu.VMEM((2 * frames, cols, tiles * LANES), f32),
            pltpu.VMEM((tiles, lags, halves, cols, LANES), f32),
            pltpu.VMEM((radii, lags, cols, LANES), f32),
            pltpu.VMEM((frames * cols, LANES), f32),
            pltpu.VMEM((side, radii, side), jnp.int32),
            pltpu.VMEM((pairs, radii * TILE, LANES), f32),
            pltpu.VMEM((radii * TILE, pairs * LANES), bf16),
            pltpu.VMEM((ext + 1, frames, LANES), bf16),
            pltpu.VMEM((ext // PACK, frames, LANES), bf16),
            pltpu.VMEM((tiles, ext, frames, LANES), bf16),
            pltpu.VMEM((cols + 2 * REACH, frames, LANES), f32),
            pltpu.VMEM((groups, frames, LANES), f32),
            pltpu.VMEM((groups, frames, LANES), bf16),
            pltpu.VMEM((groups + 2, frames, LANES), f32),
            pltpu.VMEM((cols + 2 * REACH, frames, LANES), f32),
            pltpu.VMEM((frames * cols, LANES), f32),
            pltpu.SemaphoreType.DMA((3,)),
            pltpu.SemaphoreType.DMA((radii,)),
            pltpu.SemaphoreType.DMA((11,)),
            pltpu.SemaphoreType.DMA((11,)),
        ],
        compiler_params=pltpu.CompilerParams(
            collective_id=0, has_side_effects=True, vmem_limit_bytes=VMEM_SHARE
        ),
    )(doppler.reshape(frames * cols, LANES), jnp.transpose(cycle_masks, (1, 0, 2)), lag_list)
    return (out / counts[:, None, None, :])[None]


def solution(mesh):
    return jax.shard_map(
        local,
        mesh=mesh,
        in_specs=(P("tm", ("patch", "space"), "row"), P(), P()),
        out_specs=P("tm", None, None, ("patch", "space"), "row"),
        check_vma=False,
    )
```

```python
import functools

import jax
import jax.numpy as jnp
from jax import lax
from jax.experimental import pallas as pl
from jax.experimental.pallas import tpu as pltpu
from jax.sharding import PartitionSpec as P

MESH = pl.DeviceIdType.MESH
RMAX = 16
LANES = 128
TILE = 32
SPAN = 2 * TILE
PACK = LANES // TILE
gaussian_taps = (0.05448868, 0.24420134, 0.40261995, 0.24420134, 0.05448868)
REACH = len(gaussian_taps) // 2
VMEM_SHARE = 60 * 2**20


def lane_iota(shape):
    return lax.broadcasted_iota(jnp.int32, shape, len(shape) - 1)


def pack_borders(blocks, side):
    group = lane_iota(blocks[0].shape) // TILE
    base = (1 - side) * TILE
    packed = None
    for k, block in enumerate(blocks):
        turned = pltpu.roll(block, lax.rem(k * TILE + base, LANES), 1)
        packed = turned if packed is None else jnp.where(group == k, turned, packed)
    return packed


def unpack_border(packed, k, side):
    base = side * (LANES - TILE)
    turned = pltpu.roll(packed, lax.rem(LANES - k * TILE + base, LANES), 1)
    lane = lane_iota(packed.shape)
    return jnp.where((lane >= base) & (lane < base + TILE), turned, jnp.zeros_like(turned))


def build_weights(radii, mask_in, bands, weights, counts, early):
    side = mask_in.shape[0]
    pairs = weights.shape[0] // LANES
    bits = mask_in[...].astype(jnp.float32).reshape(side * radii, side).astype(jnp.bfloat16)
    rows = lax.broadcasted_iota(jnp.int32, (side, LANES), 0)
    lane = lane_iota((side, LANES))
    put = [jnp.where(lane == rows + k * SPAN, 1.0, 0.0).astype(jnp.bfloat16) for k in range(2)]
    even, odd = [jnp.dot(bits, p, preferred_element_type=jnp.float32) for p in put]
    pieces = []
    for g in range(pairs):
        a = 2 * g
        piece = even[a * radii : (a + 1) * radii]
        if a + 1 < side:
            piece = piece + odd[(a + 1) * radii : (a + 2) * radii]
        pieces.append(piece)
    total = functools.reduce(lambda x, y: x + y, pieces)
    counts[...] = jnp.broadcast_to(jnp.sum(total, axis=1, keepdims=True), counts.shape)

    def build(some):
        for g in some:
            for q in range(TILE):
                bands[g, pl.ds(q, radii, stride=TILE), :] = pltpu.roll(pieces[g], q, 1) if q else pieces[g]
            weights[pl.ds(g * LANES, LANES), :] = bands[g].T.astype(weights.dtype)

    build(range(early))
    return lambda: build(range(early, pairs))


def build_windows(places, frames, total_cols, side, field, halo, windows):
    lane = lane_iota((frames, LANES))
    tiles = windows.shape[0]
    sources = {}

    def source(i, j):
        if i not in sources:
            own = field[i].astype(jnp.float32)
            other = jnp.zeros_like(own)
            if i < total_cols:
                other = unpack_border(halo[i // PACK].astype(jnp.float32), i % PACK, side)
            mixed = [own] * tiles
            mixed[0] = jnp.where(lane >= LANES - RMAX, other, own)
            mixed[-1] = jnp.where(lane < RMAX, other, own)
            sources[i] = mixed
        return sources[i][j]

    for i in places:
        for j in range(tiles):
            shift = (RMAX - TILE * j) % LANES
            first = pltpu.roll(source(i, j), shift, 1)
            second = pltpu.roll(source(i + 1, j), (shift + SPAN) % LANES, 1)
            windows[j, i] = jnp.where(lane < SPAN, first, second).astype(windows.dtype)


def body(frames, cols, radii, lags, dop_far, mask_far, lag_far, out_far, sums, counts, series, lag_list, spread, parts,
         out, dop, mask_in, bands, weights, field, halo, windows, wide, packs, packed16, halo_in, unpacked, natural,
         local_sem, out_sem, send, recv):
    fetch_dop = pltpu.make_async_copy(dop_far, dop, local_sem.at[0])
    fetch_mask = pltpu.make_async_copy(mask_far, mask_in, local_sem.at[1])
    fetch_dop.start()
    fetch_mask.start()
    fetch_lags = pltpu.make_async_copy(lag_far, lag_list, local_sem.at[2])
    fetch_lags.start()
    count_s, count_t = lax.axis_size("space"), lax.axis_size("tm")
    s, t, side = lax.axis_index("space"), lax.axis_index("tm"), lax.axis_index("row")
    has_lo, has_hi = s > 0, s < count_s - 1
    has_pr, has_nx = t > 0, t < count_t - 1
    lo, hi = {"space": s - 1}, {"space": s + 1}
    lo_x, hi_x = {"space": s - 1, "row": 1 - side}, {"space": s + 1, "row": 1 - side}
    partner = {"row": 1 - side}
    prev, nxt = {"tm": t - 1}, {"tm": t + 1}
    groups = cols // PACK
    reach_groups = RMAX // PACK
    top = RMAX + cols
    sent = frames * cols
    always = None

    def when(cond, act):
        if cond is None:
            act()
        else:
            pl.when(cond)(act)

    barrier = pltpu.get_barrier_semaphore()

    def greet(*devices):
        def act():
            for device in devices:
                pl.semaphore_signal(barrier, inc=1, device_id=device, device_id_type=MESH)
        return act

    greet(partner)()
    pl.when(has_lo)(greet(lo, lo_x))
    pl.when(has_hi)(greet(hi, hi_x))
    pl.when(has_pr)(greet(prev))
    pl.when(has_nx)(greet(nxt))

    fetch_dop.wait()
    for c in range(cols):
        wide[REACH + c] = dop[pl.ds(c, frames, stride=cols), :]
    for g in range(groups):
        packs[g] = pack_borders([wide[REACH + g * PACK + k] for k in range(PACK)], side)

    def zero(ref, start, size):
        def act():
            ref[pl.ds(start, size)] = jnp.zeros((size,) + ref.shape[1:], ref.dtype)
        return act

    no_lo, no_hi, no_pr = s == 0, s == count_s - 1, t == 0
    field[pl.ds(top + RMAX, 1)] = jnp.zeros((1, frames, LANES), field.dtype)
    for cond, low in ((no_lo, True), (no_hi, False)):
        pl.when(cond)(zero(wide, 0 if low else REACH + cols, REACH))
        pl.when(cond)(zero(halo_in, 0 if low else groups + 1, 1))
        pl.when(cond)(zero(field, 0 if low else top, RMAX))
        pl.when(cond)(zero(halo, 0 if low else reach_groups + groups, reach_groups))
    pl.when(no_pr)(zero(series, 0, sent))

    def copy(index, source, target, device):
        return pltpu.make_async_remote_copy(
            src_ref=source, dst_ref=target, send_sem=send.at[index], recv_sem=recv.at[index],
            device_id=device, device_id_type=MESH,
        )

    first = [
        (copy(0, wide.at[pl.ds(REACH, REACH)], wide.at[pl.ds(REACH + cols, REACH)], lo), has_lo, has_hi),
        (copy(1, wide.at[pl.ds(cols, REACH)], wide.at[pl.ds(0, REACH)], hi), has_hi, has_lo),
        (copy(2, packs, halo_in.at[pl.ds(1, groups)], partner), always, always),
        (copy(3, packs.at[pl.ds(0, 1)], halo_in.at[pl.ds(groups + 1, 1)], lo_x), has_lo, has_hi),
        (copy(4, packs.at[pl.ds(groups - 1, 1)], halo_in.at[pl.ds(0, 1)], hi_x), has_hi, has_lo),
    ]
    second = [
        (copy(5, field.at[pl.ds(RMAX, RMAX)], field.at[pl.ds(top, RMAX)], lo), has_lo, has_hi),
        (copy(6, field.at[pl.ds(cols, RMAX)], field.at[pl.ds(0, RMAX)], hi), has_hi, has_lo),
        (copy(7, packed16, halo.at[pl.ds(reach_groups, groups)], partner), always, always),
        (copy(8, packed16.at[pl.ds(0, reach_groups)],
              halo.at[pl.ds(reach_groups + groups, reach_groups)], lo_x), has_lo, has_hi),
        (copy(9, packed16.at[pl.ds(groups - reach_groups, reach_groups)],
              halo.at[pl.ds(0, reach_groups)], hi_x), has_hi, has_lo),
        (copy(10, series.at[pl.ds(sent, sent)], series.at[pl.ds(0, sent)], nxt), has_nx, has_pr),
    ]

    def spread_frames(start):
        size = LANES // TILE * LANES
        rows = lax.broadcasted_iota(jnp.int32, (LANES, size), 0)
        places = lax.broadcasted_iota(jnp.int32, (LANES, size), 1)
        pick = jnp.where(rows == (places // LANES) * TILE + places % TILE, 1.0, 0.0).astype(series.dtype)
        chosen = jnp.dot(series[pl.ds(start, frames * cols)], pick, preferred_element_type=jnp.float32)
        spread[pl.ds(start // cols, frames)] = chosen.reshape(frames, cols, size)

    met = lambda flag: jnp.where(flag, 1, 0).astype(jnp.int32)
    pl.semaphore_wait(barrier, 1 + 2 * met(has_lo) + 2 * met(has_hi) + met(has_pr) + met(has_nx))
    for moved, sends, _ in first:
        when(sends, moved.start)
    fetch_mask.wait()
    fetch_lags.wait()
    pairs = weights.shape[0] // LANES
    finish_weights = build_weights(radii, mask_in, bands, weights, counts, pairs // 3)
    for moved, _, receives in first:
        when(receives, moved.wait_recv)

    for i in range(cols + 2 * REACH):
        place = i + PACK - REACH
        unpacked[i] = unpack_border(halo_in[place // PACK], place % PACK, side)
    lane = lane_iota((frames, LANES))
    for g in range(groups):
        smoothed = []
        for k in range(PACK):
            c = g * PACK + k
            own, other = [
                functools.reduce(lambda a, b: a + b, [gaussian_taps[i] * ref[c + i] for i in range(len(gaussian_taps))])
                for ref in (wide, unpacked)
            ]
            total = None
            for i, tap in enumerate(gaussian_taps):
                shift = i - REACH
                if shift > 0:
                    moved = pltpu.roll(jnp.where(lane < shift, other, own), LANES - shift, 1)
                elif shift < 0:
                    moved = pltpu.roll(jnp.where(lane >= LANES + shift, other, own), -shift, 1)
                else:
                    moved = own
                total = tap * moved if total is None else total + tap * moved
            smoothed.append(total)
            field[RMAX + c] = total.astype(field.dtype)
            natural[pl.ds(c, frames, stride=cols), :] = total
        packed16[g] = pack_borders(smoothed, side).astype(packed16.dtype)
    series[pl.ds(sent, sent)] = natural[...].astype(series.dtype)

    for moved, sends, _ in second:
        when(sends, moved.start)
    spread_frames(frames * cols)
    finish_weights()
    for moved, sends, _ in first:
        when(sends, moved.wait_send)
    second[2][0].wait_recv()
    build_windows(range(RMAX, top - 1), frames, top + RMAX, side, field, halo, windows)

    tiles, halves = sums.shape[:2]
    block = 8
    rows = block * frames

    def products(start, chosen):
        left = jnp.concatenate(
            [
                jnp.concatenate(
                    [windows[j, pl.ds(start + 2 * g, block)].reshape(rows, LANES) for g in chosen], axis=1
                )
                for j in range(tiles)
            ],
            axis=0,
        )
        right = jnp.concatenate([weights[pl.ds(g * LANES, LANES), :] for g in chosen], axis=0)
        return jnp.dot(left, right, preferred_element_type=jnp.float32)

    def inside(start, g):
        return start + 2 * g >= RMAX and start + 2 * g + block <= top - 1

    for own in (True, False):
        for start in range(0, cols, block):
            total = products(start, [g for g in range(pairs) if inside(start, g) == own])
            for j in range(tiles):
                for h in range(halves):
                    piece = total[j * rows : (j + 1) * rows, h * LANES : (h + 1) * LANES]
                    place = pl.ds(start * frames, rows)
                    sums[j, h, place, :] = piece if own else sums[j, h, place, :] + piece
            if not own:
                correlate(start, block, frames, lags, lag_list, sums, spread, parts)
        if own:
            for moved, _, receives in second[:2] + second[3:]:
                when(receives, moved.wait_recv)
            rest = list(range(RMAX)) + list(range(top - 1, top + RMAX))
            build_windows(rest, frames, top + RMAX, side, field, halo, windows)
            spread_frames(0)

    assemble(radii, lags, counts, parts, out, out_far, out_sem)
    for moved, sends, _ in second:
        when(sends, moved.wait_send)


def correlate(start, block, frames, lags, lag_list, sums, spread, parts):
    tiles, halves = sums.shape[:2]
    starts = [frames - lag_list[l] for l in range(lags)]
    for j in range(tiles):
        totals = [[None] * halves for _ in range(lags)]
        for t in range(frames):
            place = pl.ds(start * frames + t, block, stride=frames)
            annulus = [sums[j, h, place, :] for h in range(halves)]
            for l in range(lags):
                earlier = spread[starts[l] + t, start : start + block, j * LANES : (j + 1) * LANES]
                for h in range(halves):
                    term = earlier * annulus[h]
                    totals[l][h] = term if t == 0 else totals[l][h] + term
        for l in range(lags):
            for h in range(halves):
                parts[j, l, h, start : start + block, :] = totals[l][h]


def assemble(radii, lags, counts, parts, out, out_far, out_sem):
    tiles, cols = parts.shape[0], parts.shape[3]
    group = lane_iota((cols, LANES)) // TILE
    for r in range(radii):
        h, rr = r // PACK, r % PACK
        count = counts[r : r + 1, 0:1]
        for l in range(lags):
            whole = None
            for j in range(tiles):
                shift = (TILE * (j - rr)) % LANES
                piece = parts[j, l, h]
                piece = pltpu.roll(piece, shift, 1) if shift else piece
                whole = piece if whole is None else jnp.where(group == j, piece, whole)
            out[r, l] = whole / count
        pltpu.make_async_copy(out.at[r], out_far.at[r], out_sem.at[r]).start()
    for r in range(radii):
        pltpu.make_async_copy(out.at[r], out_far.at[r], out_sem.at[r]).wait()


def local(doppler, cycle_masks, lag_list):
    frames, cols, rows = doppler.shape
    radii, side = cycle_masks.shape[:2]
    lags = lag_list.shape[0]
    assert rows == LANES and frames == RMAX and side == 2 * RMAX + 1 and cols % 8 == 0 and cols >= RMAX
    assert lax.axis_size("row") == 2 and radii % 8 == 0 and radii * TILE % LANES == 0
    groups = cols // PACK
    ext = cols + 2 * RMAX
    tiles, halves = LANES // TILE, radii * TILE // LANES
    pairs = (side + 1) // 2
    f32, bf16 = jnp.float32, jnp.bfloat16
    vmem = pl.BlockSpec(memory_space=pltpu.VMEM)
    far = pl.BlockSpec(memory_space=pltpu.HBM)
    out = pl.pallas_call(
        functools.partial(body, frames, cols, radii, lags),
        out_shape=jax.ShapeDtypeStruct((radii, lags, cols, LANES), f32),
        in_specs=[far, far, far],
        out_specs=far,
        scratch_shapes=[
            pltpu.VMEM((tiles, halves, cols * frames, LANES), f32),
            pltpu.VMEM((radii, LANES), f32),
            pltpu.VMEM((2 * frames * cols, LANES), bf16),
            pltpu.SMEM((lags,), jnp.int32),
            pltpu.VMEM((2 * frames, cols, tiles * LANES), f32),
            pltpu.VMEM((tiles, lags, halves, cols, LANES), f32),
            pltpu.VMEM((radii, lags, cols, LANES), f32),
            pltpu.VMEM((frames * cols, LANES), f32),
            pltpu.VMEM((side, radii, side), jnp.int32),
            pltpu.VMEM((pairs, radii * TILE, LANES), f32),
            pltpu.VMEM((pairs * LANES, radii * TILE), bf16),
            pltpu.VMEM((ext + 1, frames, LANES), bf16),
            pltpu.VMEM((ext // PACK, frames, LANES), bf16),
            pltpu.VMEM((tiles, ext, frames, LANES), bf16),
            pltpu.VMEM((cols + 2 * REACH, frames, LANES), f32),
            pltpu.VMEM((groups, frames, LANES), f32),
            pltpu.VMEM((groups, frames, LANES), bf16),
            pltpu.VMEM((groups + 2, frames, LANES), f32),
            pltpu.VMEM((cols + 2 * REACH, frames, LANES), f32),
            pltpu.VMEM((frames * cols, LANES), f32),
            pltpu.SemaphoreType.DMA((3,)),
            pltpu.SemaphoreType.DMA((radii,)),
            pltpu.SemaphoreType.DMA((11,)),
            pltpu.SemaphoreType.DMA((11,)),
        ],
        compiler_params=pltpu.CompilerParams(
            collective_id=0, has_side_effects=True, vmem_limit_bytes=VMEM_SHARE
        ),
    )(doppler.reshape(frames * cols, LANES), jnp.transpose(cycle_masks, (1, 0, 2)), lag_list)
    return out[None]


def solution(mesh):
    return jax.shard_map(
        local,
        mesh=mesh,
        in_specs=(P("tm", ("patch", "space"), "row"), P(), P()),
        out_specs=P("tm", None, None, ("patch", "space"), "row"),
        check_vma=False,
    )
```
